32 devices in a mesh: slide: 2 (over y), row: 8 (over z, x), col: 2 (over core).
Axes of the slice: x: 2, y: 2, z: 4, core: 2. Of those that a mesh axis runs over, the one named last changes fastest.
Arguments:
- nodes: bfloat16 [16384, 512], P(('slide', 'row', 'col')), parts along dimension 0, may hold values from -6 to 6
- ln_gain: float32 [512], replicated, may hold values from 0.1 to 1.9
- w_query: bfloat16 [512, 512], replicated, may hold values from -0.25 to 0.25
- w_key: bfloat16 [512, 512], replicated, may hold values from -0.25 to 0.25
- w_value: bfloat16 [512, 512], replicated, may hold values from -0.25 to 0.25
- w_out: bfloat16 [512, 512], replicated, may hold values from -0.25 to 0.25
- agg_gain: float32 [512], replicated, may hold values from 0.1 to 1.9
- tile_weight: bfloat16 [16, 128, 128, 128], P(('slide', 'row'), 'col'), parts along dimension 0, may hold values from 0 to 2
- tile_src: int32 [16, 128], P(('slide', 'row'), 'col'), parts along dimension 0, may hold values from 0 to 7
- tile_dst: int32 [16, 128], P(('slide', 'row'), 'col'), parts along dimension 0, may hold values from 0 to 19, as said below
- tile_live: int32 [16, 2], P(('slide', 'row'), 'col'), parts along dimension 0, may hold values from 16 to 64, as said below
Outputs:
- updated: bfloat16 [16384, 512], P(('slide', 'row', 'col')), parts along dimension 0
The draws below stay inside these ranges and needn't reach their ends.
There are 2 independent parts, one for each index of `slide`. The reference program is written for one: setup_inputs(seed, part) draws one part's arguments, and reference() takes and returns one part's arrays. A program takes and returns all parts, laid end to end along the dimension named above; an argument that names none is the same for every part. Nothing has to cross between parts.
Inputs may be any that keep to these rules, and one draw needn't show every extreme that they name: A tile on device row i targets device row i + tile_dst // 4 - 2, which always lies in the grid. `tile_live`: some device of each slide has all 64 tiles live.
All inputs are finite; a program needn't handle non-finite values.
Results may differ from the reference program's by a relative error of at most 0.006.
Values may be sent and summed in bfloat16 or wider, within the bound.
No kernel may reach another device: no remote copies, remote signals or barrier semaphores. Data moves between devices by JAX's collectives and lax.ppermute only.
A program may use at most 64 MiB of HBM per device.

```python
import math
import jax
import jax.numpy as jnp
from jax import lax

D = 512
HEADS = 8
BS = 128
HALO = 2
NB_DEV = 4
TILES_DEV = 64
NODES = 8192
N_ROW = 8
N_COL = 2


def draw_tile_weight(key, part):
    key = jax.random.fold_in(key, 11)
    first, second = jax.random.split(key)
    shape = (N_ROW, N_COL * TILES_DEV, BS, BS)
    linked = jax.random.randint(first, shape, 0, 16) == 0
    strength = jax.random.uniform(second, shape, jnp.float32, 0.5, 1.5)
    return jnp.where(linked, strength, 0.0).astype(jnp.float32).astype(jnp.bfloat16)


def draw_tile_dst(key, part):
    key = jax.random.fold_in(key, 23)
    first, second = jax.random.split(key)
    shape = (N_ROW, N_COL * TILES_DEV)
    offset = jax.random.randint(first, shape, -HALO, HALO + 1)
    row_place = lax.broadcasted_iota(jnp.int32, shape, 0)
    offset = jnp.clip(row_place + offset, 0, N_ROW - 1) - row_place
    target_block = jax.random.randint(second, shape, 0, NB_DEV)
    return ((offset + HALO) * NB_DEV + target_block).astype(jnp.int32)


def draw_tile_live(key, part):
    key = jax.random.fold_in(key, 37)
    first, second = jax.random.split(key)
    levels = jax.random.randint(first, (N_ROW, N_COL), 2, 9)
    live = TILES_DEV * levels // 8
    busiest = jax.random.randint(second, (), 0, N_ROW * N_COL)
    flat_place = jnp.arange(N_ROW * N_COL, dtype=jnp.int32).reshape(N_ROW, N_COL)
    return jnp.where(flat_place == busiest, TILES_DEV, live).astype(jnp.int32)


def with_ends(result, stream_key, low, high):
    extent = result.shape
    index_at = [jax.random.randint(jax.random.fold_in(stream_key, axis), (), 0, extent[axis]) for axis in range(len(extent))]
    result = result.at[tuple(index_at)].set(low)
    longest = extent.index(max(extent))
    index_at[longest] = (index_at[longest] + 1) % extent[longest]
    return result.at[tuple(index_at)].set(high)


def shard_levels(rng, dims, cuts, smallest, largest):
    level, own = 1.0, jax.random.fold_in(rng, 6)
    for position, shards_of in cuts:
        draws = jnp.exp(jax.random.uniform(jax.random.fold_in(own, position), (shards_of,), jnp.float32, smallest / len(cuts), largest / len(cuts)))
        level = level * jnp.repeat(draws, dims[position] // shards_of).reshape([-1 if axis == position else 1 for axis in range(len(dims))])
    return level


def scatter_about(own_key, extent, deviation, most, shards=(), held_as=jnp.bfloat16):
    drawn = jax.random.normal(own_key, extent, jnp.float32) * deviation
    if len(shards) > 0:
        drawn = shard_levels(own_key, extent, shards, -0.22, 0.18) * drawn
    return jnp.clip(drawn, min=-most, max=most).astype(held_as)


def setup_inputs(seed: int = 0, part: int = 0) -> dict:
    splits = jax.random.split(jax.random.key(seed), 12)
    own_keys = jax.random.split(jax.random.fold_in(splits[11], part), 12)
    nodes = scatter_about(own_keys[0], (NODES, D), 1.0, 6.0, ((0, 16),))
    ln_gain = jnp.clip(1.0 + 0.18 * jax.random.normal(splits[1], (D,), jnp.float32), 0.1, 1.9)
    w_query = scatter_about(splits[2], (D, D), D ** -0.5, 0.25)
    w_key = scatter_about(splits[3], (D, D), D ** -0.5, 0.25)
    w_value = scatter_about(splits[4], (D, D), D ** -0.5, 0.25)
    w_out = scatter_about(splits[5], (D, D), D ** -0.5, 0.25)
    agg_gain = jnp.clip(1.0 + 0.18 * jax.random.normal(splits[6], (D,), jnp.float32), 0.1, 1.9)
    tile_weight = draw_tile_weight(jax.random.fold_in(jax.random.fold_in(splits[11], part), 71), part)
    tile_src = with_ends(jax.random.randint(own_keys[8], (N_ROW, N_COL * TILES_DEV), 0, N_COL * NB_DEV), jax.random.fold_in(own_keys[8], 1), 0, (N_COL * NB_DEV) - 1).astype(jnp.int32)
    tile_dst = draw_tile_dst(jax.random.fold_in(jax.random.fold_in(splits[11], part), 71), part)
    tile_live = draw_tile_live(jax.random.fold_in(jax.random.fold_in(splits[11], part), 71), part)
    return dict(nodes=nodes, ln_gain=ln_gain, w_query=w_query, w_key=w_key, w_value=w_value, w_out=w_out, agg_gain=agg_gain, tile_weight=tile_weight, tile_src=tile_src, tile_dst=tile_dst, tile_live=tile_live)


epsilon_norm = 1e-05

def rms_scale(features, gain):
    features = features.astype(jnp.float32)
    scale = lax.rsqrt(lax.optimization_barrier(jnp.mean(features * features, axis=-1, keepdims=True)) + epsilon_norm)
    return features * scale * gain.astype(jnp.float32)

def tile_messages(query_tiles, key_tiles, value_tiles, weights):
    tile_count, tile_rows, features = query_tiles.shape
    head_dim = features // HEADS
    queries_4d = query_tiles.astype(jnp.float32).reshape(tile_count, tile_rows, HEADS, head_dim)
    keys_4d = key_tiles.astype(jnp.float32).reshape(tile_count, tile_rows, HEADS, head_dim)
    values_4d = value_tiles.astype(jnp.float32).reshape(tile_count, tile_rows, HEADS, head_dim)
    scores = jnp.einsum('tqhd,tkhd->thqk', queries_4d, keys_4d) * (1.0 / math.sqrt(head_dim))
    gate = (weights[:, None] * jax.nn.sigmoid(scores)).astype(jnp.bfloat16)
    merged = jnp.einsum('thqk,tkhd->tqhd', gate.astype(jnp.float32), values_4d)
    return merged.reshape(tile_count, tile_rows, features)

def reference(nodes, ln_gain, w_query, w_key, w_value, w_out, agg_gain, tile_weight, tile_src, tile_dst, tile_live):
    normed = rms_scale(nodes, ln_gain).astype(jnp.bfloat16)
    query = jnp.dot(normed, w_query, preferred_element_type=jnp.float32).astype(jnp.bfloat16).reshape(-1, BS, D)
    keys = jnp.dot(normed, w_key, preferred_element_type=jnp.float32).astype(jnp.bfloat16).reshape(-1, BS, D)
    values = jnp.dot(normed, w_value, preferred_element_type=jnp.float32).astype(jnp.bfloat16).reshape(-1, BS, D)
    device_count = N_ROW * N_COL
    weights = tile_weight.reshape(device_count, TILES_DEV, BS, BS)
    sources = tile_src.reshape(device_count, TILES_DEV).astype(jnp.int32)
    targets = tile_dst.reshape(device_count, TILES_DEV).astype(jnp.int32)
    live = tile_live.reshape(device_count).astype(jnp.int32)

    def visit(summed, inputs):
        device_place, weight, source, target, live_count = inputs
        row_index = device_place // N_COL
        col_index = device_place % N_COL
        source_block = (row_index * N_COL + source // NB_DEV) * NB_DEV + source % NB_DEV
        target_block = ((row_index + target // NB_DEV - HALO) * N_COL + col_index) * NB_DEV + target % NB_DEV
        alive_mask = (jnp.arange(TILES_DEV, dtype=jnp.int32) < live_count).astype(jnp.float32)
        weight = weight.astype(jnp.float32) * alive_mask[:, None, None]
        messages = tile_messages(query[target_block], keys[source_block], values[source_block], weight)
        return (summed.at[target_block].add(messages), None)
    summed = jnp.zeros((NODES // BS, BS, D), jnp.float32)
    summed, _ = lax.scan(visit, summed, (jnp.arange(device_count, dtype=jnp.int32), weights, sources, targets, live))
    aggregate = summed.reshape(NODES, D)
    mixed = rms_scale(aggregate, agg_gain).astype(jnp.bfloat16)
    return (nodes.astype(jnp.float32) + jnp.dot(mixed, w_out, preferred_element_type=jnp.float32)).astype(jnp.bfloat16)
```

```python
import functools

import jax
import jax.numpy as jnp
from jax import lax
from jax.experimental import pallas as pl
from jax.experimental.pallas import tpu as pltpu
from jax.sharding import PartitionSpec as P

HEADS = 8
HALO = 2
UNROLL = 4
EPSILON = 1e-05
BF16 = jnp.bfloat16
F32 = jnp.float32
VMEM = pl.BlockSpec(memory_space=pltpu.VMEM)
SMEM = pl.BlockSpec(memory_space=pltpu.SMEM)


def along(block, axis, distance):
    count = lax.axis_size(axis)
    route = [(i, i + distance) for i in range(count) if 0 <= i + distance < count]
    return lax.ppermute(block, axis, route)


def swap(block, axis, first):
    count = lax.axis_size(axis)
    pairs = [(i, i + 1) for i in range(first, count - 1, 2)]
    return lax.ppermute(block, axis, pairs + [(j, i) for i, j in pairs])


def rms_scale(features, gain):
    features = features.astype(F32)
    scale = lax.rsqrt(jnp.mean(features * features, axis=-1, keepdims=True) + EPSILON)
    return features * scale * gain


def project(normed, weight_ref):
    return jnp.dot(normed, weight_ref[...], preferred_element_type=F32).astype(BF16)


def split_heads(block):
    lane = lax.broadcasted_iota(jnp.int32, block.shape, 1)
    first = lane < block.shape[1] // 2
    zero = jnp.zeros_like(block)
    return jnp.concatenate([jnp.where(first, block, zero), jnp.where(first, zero, block)], axis=0)


def store_queries(query, query_ref):
    query = query * BF16(1.0 / 16.0)
    rows = query_ref.shape[1]
    for block in range(query_ref.shape[0]):
        query_ref[block] = query[block * rows : (block + 1) * rows]


def visit_tiles(code, src_ref, dst_ref, live_ref, weight_ref, query_ref, key_ref, value_ref, acc_ref, list_ref):
    blocks = query_ref.shape[0]
    pairs = key_ref.shape[1]
    wide = key_ref.shape[3]
    acc_ref[...] = jnp.zeros_like(acc_ref)

    def collect(tile, found):
        list_ref[found] = tile
        return found + (dst_ref[0, tile] // blocks == code).astype(jnp.int32)

    found = lax.fori_loop(0, live_ref[0, 0], collect, 0)
    for extra in range(UNROLL):
        list_ref[found + extra] = 0

    def step(index, carry):
        tiles, gates = [], []
        for u in range(UNROLL):
            place = index * UNROLL + u
            tile = list_ref[place]
            source, target = src_ref[0, tile], dst_ref[0, tile] % blocks
            half = jnp.where(place < found, 0.5, 0.0)
            weight = (weight_ref[tile].astype(F32) * half).astype(BF16)
            weight = jnp.concatenate([weight, weight], axis=1)
            tiles.append((source, target))
            gate = []
            for pair in range(pairs):
                scores = lax.dot_general(
                    query_ref[target, :, pair * wide : (pair + 1) * wide],
                    key_ref[source, pair],
                    (((1,), (1,)), ((), ())),
                    preferred_element_type=F32,
                )
                gate.append(jnp.tanh(scores.astype(BF16)) * weight + weight)
            gates.append(gate)
        sums = [
            [jnp.dot(gate[pair], value_ref[source, pair], preferred_element_type=F32) for pair in range(pairs)]
            for (source, _), gate in zip(tiles, gates)
        ]
        for (_, target), total in zip(tiles, sums):
            for pair in range(pairs):
                acc_ref[target, :, pair * wide : (pair + 1) * wide] += total[pair]
        return carry

    lax.fori_loop(0, pl.cdiv(found, UNROLL), step, 0)


def pack_heads(full, packed_ref, base):
    rows = packed_ref.shape[2] // 2
    wide = packed_ref.shape[3]
    for block in range(full.shape[0] // rows):
        for pair in range(packed_ref.shape[1]):
            packed_ref[base + block, pair] = split_heads(
                full[block * rows : (block + 1) * rows, pair * wide : (pair + 1) * wide]
            )


def own_kernel(
    src_ref, dst_ref, live_ref, nodes_ref, other_ref, gain_ref, wq_ref, wk_ref, wv_ref, weight_ref,
    out_ref, key_ref, value_ref, query_ref, list_ref,
):
    me = lax.axis_index("col")
    blocks = out_ref.shape[0]
    normed = rms_scale(nodes_ref[...], gain_ref[...]).astype(BF16)
    store_queries(project(normed, wq_ref), query_ref)
    pack_heads(project(normed, wk_ref), key_ref, me * blocks)
    pack_heads(project(normed, wv_ref), value_ref, me * blocks)
    normed = rms_scale(other_ref[...], gain_ref[...]).astype(BF16)
    pack_heads(project(normed, wk_ref), key_ref, (1 - me) * blocks)
    pack_heads(project(normed, wv_ref), value_ref, (1 - me) * blocks)
    visit_tiles(
        HALO, src_ref, dst_ref, live_ref, weight_ref, query_ref, key_ref, value_ref, out_ref, list_ref
    )


def far_kernel(
    places, src_ref, dst_ref, live_ref, gain_ref, wq_ref, weight_ref, key_ref, value_ref, *refs
):
    count = len(places)
    node_refs, out_refs = refs[:count], refs[count : 2 * count]
    query_ref, acc_ref, list_ref = refs[2 * count :]
    odd = lax.axis_index("row") % 2
    for place, nodes_ref, out_ref in zip(places, node_refs, out_refs):
        code = HALO + (place if isinstance(place, int) else jnp.where(odd == place[0], 1, -1))
        store_queries(project(rms_scale(nodes_ref[...], gain_ref[...]).astype(BF16), wq_ref), query_ref)
        visit_tiles(
            code, src_ref, dst_ref, live_ref, weight_ref, query_ref, key_ref, value_ref, acc_ref, list_ref
        )
        for block in range(acc_ref.shape[0]):
            rows = acc_ref.shape[1]
            out_ref[block * rows : (block + 1) * rows] = acc_ref[block].astype(BF16)


def last_kernel(nodes_ref, gain_ref, w_out_ref, own_ref, a_ref, b_ref, c_ref, d_ref, out_ref):
    aggregate = own_ref[...].reshape(a_ref.shape) + a_ref[...].astype(F32) + b_ref[...].astype(F32)
    aggregate = aggregate + c_ref[...].astype(F32) + d_ref[...].astype(F32)
    mixed = rms_scale(aggregate, gain_ref[...]).astype(BF16)
    update = jnp.dot(mixed, w_out_ref[...], preferred_element_type=F32)
    out_ref[...] = (nodes_ref[...].astype(F32) + update).astype(BF16)


def local(nodes, ln_gain, w_query, w_key, w_value, w_out, agg_gain, tile_weight, tile_src, tile_dst, tile_live):
    rows_dev, features = nodes.shape
    tile_count, tile_rows = tile_weight.shape[1], tile_weight.shape[-1]
    blocks = rows_dev // tile_rows
    pairs = HEADS // 2
    wide = features // pairs
    sources = lax.axis_size("col") * blocks
    gain = ln_gain.reshape(1, features)
    weight = tile_weight[0]
    params = pltpu.CompilerParams(vmem_limit_bytes=40 << 20)

    def cost(groups):
        tile_flops = 4 * tile_rows * tile_rows * features * tile_count // 5
        return pl.CostEstimate(
            flops=groups * (4 * tile_flops + 2 * rows_dev * features * features),
            bytes_accessed=8 << 20,
            transcendentals=groups * HEADS * tile_rows * tile_rows * tile_count // 5,
        )

    query_scratch = pltpu.VMEM((blocks, tile_rows, features), BF16)
    list_scratch = pltpu.SMEM((tile_count + UNROLL,), jnp.int32)
    packed = jax.ShapeDtypeStruct((sources, pairs, 2 * tile_rows, wide), BF16)
    partial_f32 = jax.ShapeDtypeStruct((blocks, tile_rows, features), F32)
    partial_bf16 = jax.ShapeDtypeStruct((rows_dev, features), BF16)

    other = lax.ppermute(nodes, "col", [(0, 1), (1, 0)])
    near = swap(nodes, "row", 0)
    above = along(nodes, "row", -HALO)
    below = along(nodes, "row", HALO)
    diagonal = swap(nodes, "row", 1)

    own, keys, values = pl.pallas_call(
        own_kernel,
        out_shape=(partial_f32, packed, packed),
        in_specs=[SMEM] * 3 + [VMEM] * 7,
        out_specs=(VMEM, VMEM, VMEM),
        scratch_shapes=[query_scratch, list_scratch],
        compiler_params=params,
        cost_estimate=cost(1),
        name="own_tiles",
    )(tile_src, tile_dst, tile_live, nodes, other, gain, w_query, w_key, w_value, weight)

    def far(name, places, blocks_in):
        return pl.pallas_call(
            functools.partial(far_kernel, places),
            out_shape=(partial_bf16,) * len(places),
            in_specs=[SMEM] * 3 + [VMEM] * (5 + len(places)),
            out_specs=(VMEM,) * len(places),
            scratch_shapes=[query_scratch, pltpu.VMEM((blocks, tile_rows, features), F32), list_scratch],
            compiler_params=params,
            cost_estimate=cost(len(places)),
            name=name,
        )(tile_src, tile_dst, tile_live, gain, w_query, weight, keys, values, *blocks_in)

    near_part, above_part, below_part = far("near_tiles", ((0,), HALO, -HALO), (near, above, below))
    near_back = swap(near_part, "row", 0)
    above_back = along(above_part, "row", HALO)
    below_back = along(below_part, "row", -HALO)
    (diagonal_part,) = far("diagonal_tiles", ((1,),), (diagonal,))
    diagonal_back = swap(diagonal_part, "row", 1)

    return pl.pallas_call(
        last_kernel,
        out_shape=jax.ShapeDtypeStruct((rows_dev, features), BF16),
        in_specs=[VMEM] * 8,
        out_specs=VMEM,
        compiler_params=params,
        cost_estimate=pl.CostEstimate(
            flops=2 * rows_dev * features * features, bytes_accessed=4 << 20, transcendentals=0
        ),
        name="mix",
    )(nodes, agg_gain.reshape(1, features), w_out, own, near_back, above_back, below_back, diagonal_back)


def solution(mesh):
    return jax.shard_map(
        local,
        mesh=mesh,
        in_specs=(
            P(("slide", "row", "col"), None),
            P(),
            P(),
            P(),
            P(),
            P(),
            P(),
            P(("slide", "row"), "col", None, None),
            P(("slide", "row"), "col"),
            P(("slide", "row"), "col"),
            P(("slide", "row"), "col"),
        ),
        out_specs=P(("slide", "row", "col"), None),
        check_vma=False,
    )
```

```python
import functools

import jax
import jax.numpy as jnp
from jax import lax
from jax.experimental import pallas as pl
from jax.experimental.pallas import tpu as pltpu
from jax.sharding import PartitionSpec as P

HEADS = 8
HALO = 2
UNROLL = 4
EPSILON = 1e-05
BF16 = jnp.bfloat16
F32 = jnp.float32
VMEM = pl.BlockSpec(memory_space=pltpu.VMEM)
SMEM = pl.BlockSpec(memory_space=pltpu.SMEM)
ANY = pl.BlockSpec(memory_space=pl.ANY)
HBM = pl.BlockSpec(memory_space=pltpu.HBM)


def swap(block, axis, stride, parity):
    count = lax.axis_size(axis)
    pairs = [(i, i + stride) for i in range(count - stride) if i // stride % 2 == parity]
    return lax.ppermute(block, axis, pairs + [(j, i) for i, j in pairs])


def partner_offset(axis, stride, parity):
    return jnp.where(lax.axis_index(axis) // stride % 2 == parity, stride, -stride)


def rms_scale(features, gain):
    features = features.astype(F32)
    scale = lax.rsqrt(jnp.mean(features * features, axis=-1, keepdims=True) + EPSILON)
    return features * scale * gain


def project(normed, weight_ref):
    return jnp.dot(normed, weight_ref[...], preferred_element_type=F32).astype(BF16)


def scaled_query(normed, weight_ref):
    return project(normed, weight_ref) * BF16(1.0 / 16.0)


def split_heads(block):
    lane = lax.broadcasted_iota(jnp.int32, block.shape, 1)
    first = lane < block.shape[1] // 2
    zero = jnp.zeros_like(block)
    return jnp.concatenate([jnp.where(first, block, zero), jnp.where(first, zero, block)], axis=0)


def pack_heads(full, packed_ref, base):
    rows = packed_ref.shape[2] // 2
    wide = packed_ref.shape[3]
    for block in range(full.shape[0] // rows):
        for pair in range(packed_ref.shape[1]):
            packed_ref[base + block, pair] = split_heads(
                full[block * rows : (block + 1) * rows, pair * wide : (pair + 1) * wide]
            )


def visit_tiles(code, list_ref, weight_ref, query_ref, key_ref, value_ref, acc_ref):
    rows = weight_ref.shape[1]
    pairs = key_ref.shape[1]
    wide = key_ref.shape[3]
    acc_ref[...] = jnp.zeros_like(acc_ref)
    found = list_ref[code, 0]

    def step(index, carry):
        tiles, gates = [], []
        for u in range(UNROLL):
            place = index * UNROLL + u
            entry = list_ref[code, 1 + place]
            tile, source, target = entry & 1023, (entry >> 10) & 1023, entry >> 20
            half = jnp.where(place < found, 0.5, 0.0)
            weight = (weight_ref[tile].astype(F32) * half).astype(BF16)
            weight = jnp.concatenate([weight, weight], axis=1)
            target = pl.ds(pl.multiple_of(target * rows, rows), rows)
            tiles.append((source, target))
            gate = []
            for pair in range(pairs):
                scores = lax.dot_general(
                    query_ref[target, pair * wide : (pair + 1) * wide],
                    key_ref[source, pair],
                    (((1,), (1,)), ((), ())),
                    preferred_element_type=F32,
                )
                gate.append(jnp.tanh(scores.astype(BF16)) * weight + weight)
            gates.append(gate)
        sums = [
            [jnp.dot(gate[pair], value_ref[source, pair], preferred_element_type=F32) for pair in range(pairs)]
            for (source, _), gate in zip(tiles, gates)
        ]
        for (_, target), total in zip(tiles, sums):
            for pair in range(pairs):
                acc_ref[target, pair * wide : (pair + 1) * wide] += total[pair]
        return carry

    lax.fori_loop(0, pl.cdiv(found, UNROLL), step, 0)


def start_copies(pairs, sems):
    copies = [pltpu.make_async_copy(a, b, sems.at[i]) for i, (a, b) in enumerate(pairs)]
    for copy in copies:
        copy.start()
    return copies


def prepare_kernel(
    blocks, src_hbm, dst_hbm, nodes_hbm, gain_hbm, wk_hbm, wv_hbm, wq_hbm, weight_hbm, live_ref, other_ref,
    key_ref, value_ref, weight_ref, nodes_ref, gain_ref, wq_ref, list_out,
    wk_ref, wv_ref, src_ref, dst_ref, list_ref, sems,
):
    copies = start_copies(
        [
            (src_hbm, src_ref), (dst_hbm, dst_ref), (nodes_hbm, nodes_ref), (gain_hbm, gain_ref), (wk_hbm, wk_ref),
            (wv_hbm, wv_ref), (wq_hbm, wq_ref), (weight_hbm, weight_ref),
        ],
        sems,
    )
    for copy in copies[:2]:
        copy.wait()
    codes = list_ref.shape[0]
    for code in range(codes):
        list_ref[code, 0] = 0

    def collect(tile, carry):
        target = dst_ref[0, tile]
        code = target // blocks
        found = list_ref[code, 0] + 1
        list_ref[code, found] = tile + src_ref[0, tile] * 1024 + (target - code * blocks) * (1024 * 1024)
        list_ref[code, 0] = found
        return carry

    lax.fori_loop(0, live_ref[0, 0], collect, 0)
    for code in range(codes):
        found = list_ref[code, 0]
        for extra in range(UNROLL):
            list_ref[code, found + 1 + extra] = 0
    list_copy = pltpu.make_async_copy(list_ref, list_out, sems.at[len(copies)])
    list_copy.start()

    me = lax.axis_index("col")
    copies[3].wait()
    other = rms_scale(other_ref[...], gain_ref[...]).astype(BF16)
    copies[2].wait()
    normed = rms_scale(nodes_ref[...], gain_ref[...]).astype(BF16)
    copies[4].wait()
    pack_heads(project(normed, wk_ref), key_ref, me * blocks)
    pack_heads(project(other, wk_ref), key_ref, (1 - me) * blocks)
    copies[5].wait()
    pack_heads(project(normed, wv_ref), value_ref, me * blocks)
    pack_heads(project(other, wv_ref), value_ref, (1 - me) * blocks)
    copies[6].wait()
    copies[7].wait()
    list_copy.wait()


def tiles_kernel(place, list_hbm, gain_ref, wq_ref, weight_ref, key_ref, value_ref, nodes_ref, _, out_ref, *scratch):
    query_ref, list_ref, sem = scratch[:3]
    copy = pltpu.make_async_copy(list_hbm, list_ref, sem)
    copy.start()
    normed = rms_scale(nodes_ref[...], gain_ref[...]).astype(BF16)
    query_ref[...] = scaled_query(normed, wq_ref)
    copy.wait()
    code = HALO + (partner_offset("row", *place) if place else 0)
    sums = out_ref if out_ref.dtype == F32 else scratch[3]
    visit_tiles(code, list_ref, weight_ref, query_ref, key_ref, value_ref, sums)
    if out_ref.dtype != F32:
        out_ref[...] = sums[...].astype(BF16)


def add_kernel(sum_ref, part_ref, out_ref):
    out_ref[...] = sum_ref[...] + part_ref[...].astype(F32)


def last_kernel(nodes_ref, gain_ref, w_out_ref, sum_ref, part_ref, out_ref):
    aggregate = sum_ref[...] + part_ref[...].astype(F32)
    mixed = rms_scale(aggregate, gain_ref[...]).astype(BF16)
    update = jnp.dot(mixed, w_out_ref[...], preferred_element_type=F32)
    out_ref[...] = (nodes_ref[...].astype(F32) + update).astype(BF16)


def local(nodes, ln_gain, w_query, w_key, w_value, w_out, agg_gain, tile_weight, tile_src, tile_dst, tile_live):
    rows_dev, features = nodes.shape
    tile_count, tile_rows = tile_weight.shape[1], tile_weight.shape[-1]
    blocks = rows_dev // tile_rows
    pairs = HEADS // 2
    wide = features // pairs
    sources = lax.axis_size("col") * blocks
    weight = tile_weight[0]
    codes = 2 * HALO + 1
    params = pltpu.CompilerParams(vmem_limit_bytes=32 << 20)

    cost = pl.CostEstimate(flops=1 << 20, bytes_accessed=1 << 16, transcendentals=0)
    shape = jax.ShapeDtypeStruct
    block_bf16 = shape((rows_dev, features), BF16)
    block_f32 = shape((rows_dev, features), F32)
    packed = shape((sources, pairs, 2 * tile_rows, wide), BF16)
    lists = (codes, 1 + tile_count + UNROLL)
    square = pltpu.VMEM((features, features), BF16)

    def in_hbm(*arrays):
        return [pltpu.with_memory_space_constraint(array, pltpu.HBM) for array in arrays]

    places = ((1, 0), (2, 0), (2, 1), (1, 1))
    other = lax.ppermute(nodes, "col", [(0, 1), (1, 0)])
    arrived = {place: swap(nodes, "row", *place) for place in places[:3]}

    keys, values, weight_held, nodes_held, gain, wq, lists_out = pl.pallas_call(
        functools.partial(prepare_kernel, blocks),
        out_shape=(
            packed, packed, shape(weight.shape, BF16), block_bf16, shape((1, features), F32),
            shape(w_query.shape, BF16), shape(lists, jnp.int32),
        ),
        in_specs=[HBM] * 8 + [SMEM, VMEM],
        out_specs=(VMEM,) * 6 + (HBM,),
        scratch_shapes=[
            square, square, pltpu.SMEM(tile_src.shape, jnp.int32), pltpu.SMEM(tile_dst.shape, jnp.int32),
            pltpu.SMEM(lists, jnp.int32), pltpu.SemaphoreType.DMA((9,)),
        ],
        compiler_params=params,
        cost_estimate=cost,
        name="prepare",
    )(
        *in_hbm(tile_src, tile_dst, nodes, ln_gain.reshape(1, features), w_key, w_value, w_query, weight),
        tile_live,
        other,
    )
    arrived[places[3]] = swap(nodes_held, "row", *places[3])

    def tiles(name, place, block, after, out):
        return pl.pallas_call(
            functools.partial(tiles_kernel, place),
            out_shape=out,
            in_specs=[HBM] + [VMEM] * 6 + [ANY],
            out_specs=VMEM,
            scratch_shapes=[
                pltpu.VMEM((rows_dev, features), BF16), pltpu.SMEM(lists, jnp.int32), pltpu.SemaphoreType.DMA,
            ] + [pltpu.VMEM((rows_dev, features), F32)] * (out.dtype != F32),
            compiler_params=params,
            cost_estimate=cost,
            name=name,
        )(lists_out, gain, wq, weight_held, keys, values, block, after)

    last, returned = gain, []
    for place in places:
        last = tiles("tiles_%d_%d" % place, place, arrived[place], last, block_bf16)
        returned.append(swap(last, "row", *place))
    total = tiles("own_tiles", None, nodes_held, last, block_f32)
    for part in returned[:-1]:
        total = pl.pallas_call(
            add_kernel,
            out_shape=block_f32,
            in_specs=[VMEM] * 2,
            out_specs=VMEM,
            input_output_aliases={0: 0},
            compiler_params=params,
            cost_estimate=pl.CostEstimate(flops=1 << 18, bytes_accessed=2 << 20, transcendentals=0),
            name="add",
        )(total, part)

    return pl.pallas_call(
        last_kernel,
        out_shape=block_bf16,
        in_specs=[VMEM] * 5,
        out_specs=VMEM,
        compiler_params=params,
        cost_estimate=cost,
        name="mix",
    )(nodes, agg_gain.reshape(1, features), w_out, total, returned[-1])


def solution(mesh):
    return jax.shard_map(
        local,
        mesh=mesh,
        in_specs=(
            P(("slide", "row", "col"), None),
            P(),
            P(),
            P(),
            P(),
            P(),
            P(),
            P(("slide", "row"), "col", None, None),
            P(("slide", "row"), "col"),
            P(("slide", "row"), "col"),
            P(("slide", "row"), "col"),
        ),
        out_specs=P(("slide", "row", "col"), None),
        check_vma=False,
    )
```

```python
import functools

import jax
import jax.numpy as jnp
from jax import lax
from jax.experimental import pallas as pl
from jax.experimental.pallas import tpu as pltpu
from jax.sharding import PartitionSpec as P

HEADS = 8
HALO = 2
UNROLL = 4
EPSILON = 1e-05
BF16 = jnp.bfloat16
F32 = jnp.float32
VMEM = pl.BlockSpec(memory_space=pltpu.VMEM)
SMEM = pl.BlockSpec(memory_space=pltpu.SMEM)
ANY = pl.BlockSpec(memory_space=pl.ANY)
HBM = pl.BlockSpec(memory_space=pltpu.HBM)


def swap(block, axis, stride, parity):
    count = lax.axis_size(axis)
    pairs = [(i, i + stride) for i in range(count - stride) if i // stride % 2 == parity]
    return lax.ppermute(block, axis, pairs + [(j, i) for i, j in pairs])


def partner_offset(axis, stride, parity):
    return jnp.where(lax.axis_index(axis) // stride % 2 == parity, stride, -stride)


def rms_scale(features, gain):
    features = features.astype(F32)
    scale = lax.rsqrt(jnp.mean(features * features, axis=-1, keepdims=True) + EPSILON)
    return features * scale * gain


def project(normed, weight_ref):
    return jnp.dot(normed, weight_ref[...], preferred_element_type=F32).astype(BF16)


def scaled_query(normed, weight_ref):
    return project(normed, weight_ref) * BF16(1.0 / 16.0)


def split_heads(block):
    lane = lax.broadcasted_iota(jnp.int32, block.shape, 1)
    first = lane < block.shape[1] // 2
    zero = jnp.zeros_like(block)
    return jnp.concatenate([jnp.where(first, block, zero), jnp.where(first, zero, block)], axis=0)


def pack_heads(full, packed_ref, base):
    rows = packed_ref.shape[2] // 2
    wide = packed_ref.shape[3]
    for block in range(full.shape[0] // rows):
        for pair in range(packed_ref.shape[1]):
            packed_ref[base + block, pair] = split_heads(
                full[block * rows : (block + 1) * rows, pair * wide : (pair + 1) * wide]
            )


def visit_tiles(code, list_ref, weight_ref, query_ref, key_ref, value_ref, acc_ref):
    rows = weight_ref.shape[1]
    pairs = key_ref.shape[1]
    wide = key_ref.shape[3]
    acc_ref[...] = jnp.zeros_like(acc_ref)
    codes = list_ref.shape[0] // 2
    found = list_ref[2 * codes, code]

    def visit(first, count):
        tiles, gates = [], []
        for place in range(count):
            place = first + place
            entry, twin = list_ref[code, place], list_ref[codes + code, place]
            tile, source, target = entry & 1023, (entry >> 10) & 1023, entry >> 20
            half = jnp.where(place < found, 0.5, 0.0)
            weight = weight_ref[tile].astype(F32) * half
            weight += weight_ref[jnp.maximum(twin - 1, 0)].astype(F32) * jnp.where(twin > 0, half, 0.0)
            weight = jnp.concatenate([weight, weight], axis=1)
            target = pl.ds(pl.multiple_of(target * rows, rows), rows)
            tiles.append((source, target))
            gate = []
            for pair in range(pairs):
                scores = lax.dot_general(
                    query_ref[target, pair * wide : (pair + 1) * wide],
                    key_ref[source, pair],
                    (((1,), (1,)), ((), ())),
                    preferred_element_type=F32,
                )
                gate.append((jnp.tanh(scores) * weight + weight).astype(BF16))
            gates.append(gate)
        sums = [
            [jnp.dot(gate[pair], value_ref[source, pair], preferred_element_type=F32) for pair in range(pairs)]
            for (source, _), gate in zip(tiles, gates)
        ]
        for (_, target), total in zip(tiles, sums):
            for pair in range(pairs):
                acc_ref[target, pair * wide : (pair + 1) * wide] += total[pair]

    many = found // (2 * UNROLL)

    @pl.loop(0, many)
    def _(index):
        visit(index * (2 * UNROLL), 2 * UNROLL)

    @pl.loop(2 * many, pl.cdiv(found, UNROLL))
    def _(index):
        visit(index * UNROLL, UNROLL)


def start_copies(pairs, sems):
    copies = [pltpu.make_async_copy(a, b, sems.at[i]) for i, (a, b) in enumerate(pairs)]
    for copy in copies:
        copy.start()
    return copies


def make_lists(blocks, source, target, live, list_ref):
    codes, tiles = list_ref.shape[0] // 2, source.shape[1]
    square = (tiles, tiles)
    down, along = lax.broadcasted_iota(jnp.int32, square, 0), lax.broadcasted_iota(jnp.int32, square, 1)
    one = lambda mask: mask.astype(jnp.int32)
    column = lambda row: jnp.sum(jnp.where(down == along, row, 0), axis=1, keepdims=True)
    source_c, target_c = column(source), column(target)
    code, code_c = target // blocks, target_c // blocks
    number, number_c = along[:1], down[:, :1]
    alike = (source == source_c) & (target == target_c)
    rank = jnp.sum(one(alike & (down < along)), axis=0, keepdims=True)
    rank_c = jnp.sum(one(alike & (along < down)), axis=1, keepdims=True)
    first, first_c = (rank % 2 == 0) & (number < live), (rank_c % 2 == 0) & (number_c < live)
    place_c = jnp.sum(one(first & (code == code_c) & (along < down)), axis=1, keepdims=True)
    twin_c = jnp.sum(
        jnp.where(alike & (rank == rank_c + 1) & (number < live), number + 1, 0), axis=1, keepdims=True
    )
    entry_c = number_c + source_c * 1024 + (target_c - code_c * blocks) * (1024 * 1024)
    lane = lax.broadcasted_iota(jnp.int32, (tiles, list_ref.shape[1]), 1)
    here = first_c & (place_c == lane)
    lengths = jnp.zeros((1, list_ref.shape[1]), jnp.int32)
    for each in range(codes):
        mine = here & (code_c == each)
        list_ref[each : each + 1] = jnp.sum(jnp.where(mine, entry_c, 0), axis=0, keepdims=True)
        list_ref[codes + each : codes + each + 1] = jnp.sum(jnp.where(mine, twin_c, 0), axis=0, keepdims=True)
        length = jnp.sum(one(first_c & (code_c == each)), axis=0, keepdims=True)
        lengths += jnp.where(lane[:1] == each, length, 0)
    list_ref[2 * codes :] = lengths


def prepare_kernel(
    blocks, src_hbm, dst_hbm, nodes_hbm, gain_hbm, wk_hbm, wv_hbm, wq_hbm, weight_hbm, live_ref, other_ref,
    key_ref, value_ref, weight_ref, query_ref, gain_ref, wq_ref, list_out,
    nodes_ref, wk_ref, wv_ref, src_ref, dst_ref, sems,
):
    copies = start_copies(
        [
            (src_hbm, src_ref), (dst_hbm, dst_ref), (nodes_hbm, nodes_ref), (gain_hbm, gain_ref), (wk_hbm, wk_ref),
            (wv_hbm, wv_ref), (wq_hbm, wq_ref), (weight_hbm, weight_ref),
        ],
        sems,
    )
    for copy in copies[:2]:
        copy.wait()
    make_lists(blocks, src_ref[...], dst_ref[...], live_ref[0, 0], list_out)
    me = lax.axis_index("col")
    copies[3].wait()
    other = rms_scale(other_ref[...], gain_ref[...]).astype(BF16)
    copies[2].wait()
    normed = rms_scale(nodes_ref[...], gain_ref[...]).astype(BF16)
    copies[4].wait()
    pack_heads(project(normed, wk_ref), key_ref, me * blocks)
    pack_heads(project(other, wk_ref), key_ref, (1 - me) * blocks)
    copies[5].wait()
    pack_heads(project(normed, wv_ref), value_ref, me * blocks)
    pack_heads(project(other, wv_ref), value_ref, (1 - me) * blocks)
    copies[6].wait()
    query_ref[...] = scaled_query(normed, wq_ref)
    copies[7].wait()


def tiles_kernel(places, list_hbm, gain_ref, wq_ref, weight_ref, key_ref, value_ref, *refs):
    count = len(places)
    block_refs, out_refs, (query_ref, acc_ref, list_ref, sem) = refs[:count], refs[count + 1 : 2 * count + 1], refs[2 * count + 1 :]
    copy = pltpu.make_async_copy(list_hbm, list_ref, sem)
    copy.start()
    for index, (place, block_ref, out_ref) in enumerate(zip(places, block_refs, out_refs)):
        code, queries = HALO, block_ref
        if place is not None:
            code = HALO + partner_offset("row", *place)
            if place != (1, 1):
                queries = query_ref
                query_ref[...] = scaled_query(rms_scale(block_ref[...], gain_ref[...]).astype(BF16), wq_ref)
        if index == 0:
            copy.wait()
        sums = out_ref if out_ref.dtype == F32 else acc_ref
        visit_tiles(code, list_ref, weight_ref, queries, key_ref, value_ref, sums)
        if out_ref.dtype != F32:
            out_ref[...] = sums[...].astype(BF16)


def add_kernel(sum_ref, part_ref, out_ref):
    out_ref[...] = sum_ref[...] + part_ref[...].astype(F32)


def last_kernel(nodes_ref, gain_ref, w_out_ref, sum_ref, part_ref, out_ref):
    aggregate = sum_ref[...] + part_ref[...].astype(F32)
    mixed = rms_scale(aggregate, gain_ref[...]).astype(BF16)
    update = jnp.dot(mixed, w_out_ref[...], preferred_element_type=F32)
    out_ref[...] = (nodes_ref[...].astype(F32) + update).astype(BF16)


def local(nodes, ln_gain, w_query, w_key, w_value, w_out, agg_gain, tile_weight, tile_src, tile_dst, tile_live):
    rows_dev, features = nodes.shape
    tile_count, tile_rows = tile_weight.shape[1], tile_weight.shape[-1]
    blocks = rows_dev // tile_rows
    pairs = HEADS // 2
    wide = features // pairs
    sources = lax.axis_size("col") * blocks
    weight = tile_weight[0]
    codes = 2 * HALO + 1
    params = pltpu.CompilerParams(vmem_limit_bytes=32 << 20)

    cost = pl.CostEstimate(flops=1 << 20, bytes_accessed=1 << 16, transcendentals=0)
    shape = jax.ShapeDtypeStruct
    block_bf16 = shape((rows_dev, features), BF16)
    block_f32 = shape((rows_dev, features), F32)
    packed = shape((sources, pairs, 2 * tile_rows, wide), BF16)
    lists = (2 * codes + 1, 128)
    assert tile_count + UNROLL <= 128 and sources <= 1024
    square = pltpu.VMEM((features, features), BF16)

    def in_hbm(*arrays):
        return [pltpu.with_memory_space_constraint(array, pltpu.HBM) for array in arrays]

    groups = [((1, 0),), ((2, 1),), ((2, 0),), ((1, 1),)]
    other = lax.ppermute(nodes, "col", [(0, 1), (1, 0)])
    arrived = {place: swap(nodes, "row", *place) for group in groups for place in group if place != (1, 1)}
    keys, values, weight_held, query, gain, wq, lists_out = pl.pallas_call(
        functools.partial(prepare_kernel, blocks),
        out_shape=(
            packed, packed, shape(weight.shape, BF16), block_bf16, shape((1, features), F32),
            shape(w_query.shape, BF16), shape(lists, jnp.int32),
        ),
        in_specs=[HBM] * 8 + [SMEM, VMEM],
        out_specs=(VMEM,) * 7,
        scratch_shapes=[
            pltpu.VMEM((rows_dev, features), BF16), square, square, pltpu.VMEM(tile_src.shape, jnp.int32),
            pltpu.VMEM(tile_dst.shape, jnp.int32), pltpu.SemaphoreType.DMA((9,)),
        ],
        compiler_params=params,
        cost_estimate=cost,
        name="prepare",
    )(
        *in_hbm(tile_src, tile_dst, nodes, ln_gain.reshape(1, features), w_key, w_value, w_query, weight),
        tile_live,
        other,
    )

    arrived[1, 1] = swap(query, "row", 1, 1)

    def tiles(name, places, blocks_in, after, out):
        return pl.pallas_call(
            functools.partial(tiles_kernel, places),
            out_shape=(out,) * len(places),
            in_specs=[VMEM] * (6 + len(places)) + [ANY],
            out_specs=(VMEM,) * len(places),
            scratch_shapes=[
                pltpu.VMEM((rows_dev, features), BF16), pltpu.VMEM((rows_dev, features), F32),
                pltpu.SMEM(lists, jnp.int32), pltpu.SemaphoreType.DMA,
            ],
            compiler_params=params,
            cost_estimate=cost,
            name=name,
        )(lists_out, gain, wq, weight_held, keys, values, *blocks_in, after)

    last, returned, total = gain, [], None
    for index, group in enumerate(groups):
        if index == 99:
            (total,) = tiles("own_tiles", (None,), (query,), last, block_f32)
            last = total
        sums = tiles("tiles_%d" % index, group, [arrived[place] for place in group], last, block_bf16)
        returned += [swap(part, "row", *place) for part, place in zip(sums, group)]
        last = sums[-1]
    if total is None:
        (total,) = tiles("own_tiles", (None,), (query,), last, block_f32)
    for part in returned[:-1]:
        total = pl.pallas_call(
            add_kernel,
            out_shape=block_f32,
            in_specs=[VMEM] * 2,
            out_specs=VMEM,
            input_output_aliases={0: 0},
            compiler_params=params,
            cost_estimate=pl.CostEstimate(flops=1 << 18, bytes_accessed=2 << 20, transcendentals=0),
            name="add",
        )(total, part)

    return pl.pallas_call(
        last_kernel,
        out_shape=block_bf16,
        in_specs=[VMEM] * 5,
        out_specs=VMEM,
        compiler_params=params,
        cost_estimate=cost,
        name="mix",
    )(nodes, agg_gain.reshape(1, features), w_out, total, returned[-1])


def solution(mesh):
    return jax.shard_map(
        local,
        mesh=mesh,
        in_specs=(
            P(("slide", "row", "col"), None),
            P(),
            P(),
            P(),
            P(),
            P(),
            P(),
            P(("slide", "row"), "col", None, None),
            P(("slide", "row"), "col"),
            P(("slide", "row"), "col"),
            P(("slide", "row"), "col"),
        ),
        out_specs=P(("slide", "row", "col"), None),
        check_vma=False,
    )
```

```python
import functools

import jax
import jax.numpy as jnp
from jax import lax
from jax.experimental import pallas as pl
from jax.experimental.pallas import tpu as pltpu
from jax.sharding import PartitionSpec as P

HEADS = 8
HALO = 2
UNROLL = 4
EPSILON = 1e-05
BF16 = jnp.bfloat16
F32 = jnp.float32
VMEM = pl.BlockSpec(memory_space=pltpu.VMEM)
SMEM = pl.BlockSpec(memory_space=pltpu.SMEM)
ANY = pl.BlockSpec(memory_space=pl.ANY)
HBM = pl.BlockSpec(memory_space=pltpu.HBM)


def swap(block, axis, stride, parity):
    count = lax.axis_size(axis)
    pairs = [(i, i + stride) for i in range(count - stride) if i // stride % 2 == parity]
    return lax.ppermute(block, axis, pairs + [(j, i) for i, j in pairs])


def partner_offset(axis, stride, parity):
    return jnp.where(lax.axis_index(axis) // stride % 2 == parity, stride, -stride)


def rms_scale(features, gain):
    features = features.astype(F32)
    scale = lax.rsqrt(jnp.mean(features * features, axis=-1, keepdims=True) + EPSILON)
    return features * scale * gain


def project(normed, weight_ref):
    return jnp.dot(normed, weight_ref[...], preferred_element_type=F32).astype(BF16)


def scaled_query(normed, weight_ref):
    return project(normed, weight_ref) * BF16(1.0 / 16.0)


def split_heads(block):
    lane = lax.broadcasted_iota(jnp.int32, block.shape, 1)
    first = lane < block.shape[1] // 2
    zero = jnp.zeros_like(block)
    return jnp.concatenate([jnp.where(first, block, zero), jnp.where(first, zero, block)], axis=0)


def pack_heads(full, packed_ref, base):
    rows = packed_ref.shape[2] // 2
    wide = packed_ref.shape[3]
    for block in range(full.shape[0] // rows):
        for pair in range(packed_ref.shape[1]):
            packed_ref[base + block, pair] = split_heads(
                full[block * rows : (block + 1) * rows, pair * wide : (pair + 1) * wide]
            )


def visit_tiles(code, list_ref, weight_ref, query_ref, key_ref, value_ref, acc_ref):
    rows = weight_ref.shape[1]
    pairs = key_ref.shape[1]
    wide = key_ref.shape[3]
    acc_ref[...] = jnp.zeros_like(acc_ref)
    codes = list_ref.shape[0] // 2
    found = list_ref[2 * codes, code]

    def visit(first, count):
        tiles, gates = [], []
        for place in range(count):
            place = first + place
            entry, twin = list_ref[code, place], list_ref[codes + code, place]
            tile, source, target = entry & 1023, (entry >> 10) & 1023, entry >> 20
            half = jnp.where(place < found, 0.5, 0.0)
            weight = weight_ref[tile].astype(F32) * half
            weight += weight_ref[jnp.maximum(twin - 1, 0)].astype(F32) * jnp.where(twin > 0, half, 0.0)
            weight = jnp.concatenate([weight, weight], axis=1)
            target = pl.ds(pl.multiple_of(target * rows, rows), rows)
            tiles.append((source, target))
            gate = []
            for pair in range(pairs):
                scores = lax.dot_general(
                    query_ref[target, pair * wide : (pair + 1) * wide],
                    key_ref[source, pair],
                    (((1,), (1,)), ((), ())),
                    preferred_element_type=F32,
                )
                gate.append((jnp.tanh(scores) * weight + weight).astype(BF16))
            gates.append(gate)
        sums = [
            [jnp.dot(gate[pair], value_ref[source, pair], preferred_element_type=F32) for pair in range(pairs)]
            for (source, _), gate in zip(tiles, gates)
        ]
        for (_, target), total in zip(tiles, sums):
            for pair in range(pairs):
                acc_ref[target, pair * wide : (pair + 1) * wide] += total[pair]

    many = found // (2 * UNROLL)

    @pl.loop(0, many)
    def _(index):
        visit(index * (2 * UNROLL), 2 * UNROLL)

    @pl.loop(2 * many, pl.cdiv(found, UNROLL))
    def _(index):
        visit(index * UNROLL, UNROLL)


def start_copies(pairs, sems):
    copies = [pltpu.make_async_copy(a, b, sems.at[i]) for i, (a, b) in enumerate(pairs)]
    for copy in copies:
        copy.start()
    return copies


def make_lists(blocks, source, target, live, list_ref):
    codes, tiles = list_ref.shape[0] // 2, source.shape[1]
    square = (tiles, tiles)
    down, along = lax.broadcasted_iota(jnp.int32, square, 0), lax.broadcasted_iota(jnp.int32, square, 1)
    one = lambda mask: mask.astype(jnp.int32)
    column = lambda row: jnp.sum(jnp.where(down == along, row, 0), axis=1, keepdims=True)
    source_c, target_c = column(source), column(target)
    code, code_c = target // blocks, target_c // blocks
    number, number_c = along[:1], down[:, :1]
    alike = (source == source_c) & (target == target_c)
    rank = jnp.sum(one(alike & (down < along)), axis=0, keepdims=True)
    rank_c = jnp.sum(one(alike & (along < down)), axis=1, keepdims=True)
    first, first_c = (rank % 2 == 0) & (number < live), (rank_c % 2 == 0) & (number_c < live)
    place_c = jnp.sum(one(first & (code == code_c) & (along < down)), axis=1, keepdims=True)
    twin_c = jnp.sum(
        jnp.where(alike & (rank == rank_c + 1) & (number < live), number + 1, 0), axis=1, keepdims=True
    )
    entry_c = number_c + source_c * 1024 + (target_c - code_c * blocks) * (1024 * 1024)
    lane = lax.broadcasted_iota(jnp.int32, (tiles, list_ref.shape[1]), 1)
    here = first_c & (place_c == lane)
    lengths = jnp.zeros((1, list_ref.shape[1]), jnp.int32)
    for each in range(codes):
        mine = here & (code_c == each)
        list_ref[each : each + 1] = jnp.sum(jnp.where(mine, entry_c, 0), axis=0, keepdims=True)
        list_ref[codes + each : codes + each + 1] = jnp.sum(jnp.where(mine, twin_c, 0), axis=0, keepdims=True)
        length = jnp.sum(one(first_c & (code_c == each)), axis=0, keepdims=True)
        lengths += jnp.where(lane[:1] == each, length, 0)
    list_ref[2 * codes :] = lengths


def prepare_kernel(
    blocks, src_hbm, dst_hbm, nodes_hbm, gain_hbm, wk_hbm, wv_hbm, wq_hbm, weight_hbm, live_ref, other_ref,
    key_ref, value_ref, weight_ref, query_ref, gain_ref, wq_ref, list_out,
    nodes_ref, wk_ref, wv_ref, src_ref, dst_ref, sems,
):
    copies = start_copies(
        [
            (src_hbm, src_ref), (dst_hbm, dst_ref), (nodes_hbm, nodes_ref), (gain_hbm, gain_ref), (wk_hbm, wk_ref),
            (wv_hbm, wv_ref), (wq_hbm, wq_ref), (weight_hbm, weight_ref),
        ],
        sems,
    )
    for copy in copies[:2]:
        copy.wait()
    make_lists(blocks, src_ref[...], dst_ref[...], live_ref[0, 0], list_out)
    me = lax.axis_index("col")
    copies[3].wait()
    other = rms_scale(other_ref[...], gain_ref[...]).astype(BF16)
    copies[2].wait()
    normed = rms_scale(nodes_ref[...], gain_ref[...]).astype(BF16)
    copies[4].wait()
    pack_heads(project(normed, wk_ref), key_ref, me * blocks)
    pack_heads(project(other, wk_ref), key_ref, (1 - me) * blocks)
    copies[5].wait()
    pack_heads(project(normed, wv_ref), value_ref, me * blocks)
    pack_heads(project(other, wv_ref), value_ref, (1 - me) * blocks)
    copies[6].wait()
    query_ref[...] = scaled_query(normed, wq_ref)
    copies[7].wait()


def tiles_kernel(
    place, projected, lists_vmem, gain_ref, wq_ref, weight_ref, key_ref, value_ref, block_ref, _, out_ref,
    query_ref, acc_ref, list_ref, sem,
):
    copy = pltpu.make_async_copy(lists_vmem, list_ref, sem)
    copy.start()
    queries = block_ref
    if not projected:
        queries = query_ref
        query_ref[...] = scaled_query(rms_scale(block_ref[...], gain_ref[...]).astype(BF16), wq_ref)
    copy.wait()
    code = HALO + (partner_offset("row", *place) if place else 0)
    sums = out_ref if out_ref.dtype == F32 else acc_ref
    visit_tiles(code, list_ref, weight_ref, queries, key_ref, value_ref, sums)
    if out_ref.dtype != F32:
        out_ref[...] = sums[...].astype(BF16)


def add_kernel(sum_ref, part_ref, out_ref):
    out_ref[...] = sum_ref[...] + part_ref[...].astype(F32)


def last_kernel(nodes_ref, gain_ref, w_out_ref, sum_ref, part_ref, out_ref):
    aggregate = sum_ref[...] + part_ref[...].astype(F32)
    mixed = rms_scale(aggregate, gain_ref[...]).astype(BF16)
    update = jnp.dot(mixed, w_out_ref[...], preferred_element_type=F32)
    out_ref[...] = (nodes_ref[...].astype(F32) + update).astype(BF16)


def local(nodes, ln_gain, w_query, w_key, w_value, w_out, agg_gain, tile_weight, tile_src, tile_dst, tile_live):
    rows_dev, features = nodes.shape
    tile_count, tile_rows = tile_weight.shape[1], tile_weight.shape[-1]
    blocks = rows_dev // tile_rows
    pairs = HEADS // 2
    wide = features // pairs
    sources = lax.axis_size("col") * blocks
    weight = tile_weight[0]
    codes = 2 * HALO + 1
    params = pltpu.CompilerParams(vmem_limit_bytes=32 << 20)

    cost = pl.CostEstimate(flops=1 << 20, bytes_accessed=1 << 16, transcendentals=0)
    shape = jax.ShapeDtypeStruct
    block_bf16 = shape((rows_dev, features), BF16)
    block_f32 = shape((rows_dev, features), F32)
    packed = shape((sources, pairs, 2 * tile_rows, wide), BF16)
    lists = (2 * codes + 1, 128)
    assert tile_count + UNROLL <= 128 and sources <= 1024
    square = pltpu.VMEM((features, features), BF16)

    def in_hbm(*arrays):
        return [pltpu.with_memory_space_constraint(array, pltpu.HBM) for array in arrays]

    near, diagonal = (1, 0), (1, 1)
    places = (near, (HALO, 1), (HALO, 0), diagonal)
    other = lax.ppermute(nodes, "col", [(0, 1), (1, 0)])
    arrived = {place: swap(nodes, "row", *place) for place in places if place != diagonal}

    keys, values, weight_held, query, gain, wq, lists_out = pl.pallas_call(
        functools.partial(prepare_kernel, blocks),
        out_shape=(
            packed, packed, shape(weight.shape, BF16), block_bf16, shape((1, features), F32),
            shape(w_query.shape, BF16), shape(lists, jnp.int32),
        ),
        in_specs=[HBM] * 8 + [SMEM, VMEM],
        out_specs=(VMEM,) * 7,
        scratch_shapes=[
            pltpu.VMEM((rows_dev, features), BF16), square, square, pltpu.VMEM(tile_src.shape, jnp.int32),
            pltpu.VMEM(tile_dst.shape, jnp.int32), pltpu.SemaphoreType.DMA((9,)),
        ],
        compiler_params=params,
        cost_estimate=cost,
        name="prepare",
    )(
        *in_hbm(tile_src, tile_dst, nodes, ln_gain.reshape(1, features), w_key, w_value, w_query, weight),
        tile_live,
        other,
    )

    arrived[diagonal] = swap(query, "row", *diagonal)

    def tiles(name, place, projected, block, after, out):
        return pl.pallas_call(
            functools.partial(tiles_kernel, place, projected),
            out_shape=out,
            in_specs=[VMEM] * 7 + [ANY],
            out_specs=VMEM,
            scratch_shapes=[
                pltpu.VMEM((rows_dev, features), BF16), pltpu.VMEM((rows_dev, features), F32),
                pltpu.SMEM(lists, jnp.int32), pltpu.SemaphoreType.DMA,
            ],
            compiler_params=params,
            cost_estimate=cost,
            name=name,
        )(lists_out, gain, wq, weight_held, keys, values, block, after)

    last, returned = gain, []
    for place in places:
        last = tiles("tiles_%d_%d" % place, place, place == diagonal, arrived[place], last, block_bf16)
        returned.append(swap(last, "row", *place))
    total = tiles("own_tiles", None, True, query, last, block_f32)
    for part in returned[:-1]:
        total = pl.pallas_call(
            add_kernel,
            out_shape=block_f32,
            in_specs=[VMEM] * 2,
            out_specs=VMEM,
            input_output_aliases={0: 0},
            compiler_params=params,
            cost_estimate=pl.CostEstimate(flops=1 << 18, bytes_accessed=2 << 20, transcendentals=0),
            name="add",
        )(total, part)

    return pl.pallas_call(
        last_kernel,
        out_shape=block_bf16,
        in_specs=[VMEM] * 5,
        out_specs=VMEM,
        compiler_params=params,
        cost_estimate=cost,
        name="mix",
    )(nodes, agg_gain.reshape(1, features), w_out, total, returned[-1])


def solution(mesh):
    return jax.shard_map(
        local,
        mesh=mesh,
        in_specs=(
            P(("slide", "row", "col"), None),
            P(),
            P(),
            P(),
            P(),
            P(),
            P(),
            P(("slide", "row"), "col", None, None),
            P(("slide", "row"), "col"),
            P(("slide", "row"), "col"),
            P(("slide", "row"), "col"),
        ),
        out_specs=P(("slide", "row", "col"), None),
        check_vma=False,
    )
```

```python
import functools

import jax
import jax.numpy as jnp
from jax import lax
from jax.experimental import pallas as pl
from jax.experimental.pallas import tpu as pltpu
from jax.sharding import PartitionSpec as P

HEADS = 8
HALO = 2
UNROLL = 4
EPSILON = 1e-05
BF16 = jnp.bfloat16
F32 = jnp.float32
VMEM = pl.BlockSpec(memory_space=pltpu.VMEM)
SMEM = pl.BlockSpec(memory_space=pltpu.SMEM)
ANY = pl.BlockSpec(memory_space=pl.ANY)
HBM = pl.BlockSpec(memory_space=pltpu.HBM)


def swap(block, axis, stride, parity):
    count = lax.axis_size(axis)
    pairs = [(i, i + stride) for i in range(count - stride) if i // stride % 2 == parity]
    return lax.ppermute(block, axis, pairs + [(j, i) for i, j in pairs])


def partner_offset(axis, stride, parity):
    return jnp.where(lax.axis_index(axis) // stride % 2 == parity, stride, -stride)


def rms_scale(features, gain):
    features = features.astype(F32)
    scale = lax.rsqrt(jnp.mean(features * features, axis=-1, keepdims=True) + EPSILON)
    return features * scale * gain


def project(normed, weight_ref):
    return jnp.dot(normed, weight_ref[...], preferred_element_type=F32).astype(BF16)


def scaled_query(normed, weight_ref):
    return project(normed, weight_ref) * BF16(1.0 / 16.0)


def split_heads(block):
    lane = lax.broadcasted_iota(jnp.int32, block.shape, 1)
    first = lane < block.shape[1] // 2
    zero = jnp.zeros_like(block)
    return jnp.concatenate([jnp.where(first, block, zero), jnp.where(first, zero, block)], axis=0)


def pack_heads(full, packed_ref, base):
    rows = packed_ref.shape[2] // 2
    wide = packed_ref.shape[3]
    for block in range(full.shape[0] // rows):
        for pair in range(packed_ref.shape[1]):
            packed_ref[base + block, pair] = split_heads(
                full[block * rows : (block + 1) * rows, pair * wide : (pair + 1) * wide]
            )


def visit_tiles(code, list_ref, weight_ref, query_ref, key_ref, value_ref, acc_ref):
    rows = weight_ref.shape[1]
    pairs = key_ref.shape[1]
    wide = key_ref.shape[3]
    acc_ref[...] = jnp.zeros_like(acc_ref)
    codes = list_ref.shape[0] // 2
    found = list_ref[2 * codes, code]

    def visit(first, count):
        tiles, gates = [], []
        for place in range(count):
            place = first + place
            entry, twin = list_ref[code, place], list_ref[codes + code, place]
            tile, source, target = entry & 1023, (entry >> 10) & 1023, entry >> 20
            half = jnp.where(place < found, 0.5, 0.0)
            weight = weight_ref[tile].astype(F32) * half
            weight += weight_ref[jnp.maximum(twin - 1, 0)].astype(F32) * jnp.where(twin > 0, half, 0.0)
            weight = jnp.concatenate([weight, weight], axis=1)
            target = pl.ds(pl.multiple_of(target * rows, rows), rows)
            tiles.append((source, target))
            gate = []
            for pair in range(pairs):
                scores = lax.dot_general(
                    query_ref[target, pair * wide : (pair + 1) * wide],
                    key_ref[source, pair],
                    (((1,), (1,)), ((), ())),
                    preferred_element_type=F32,
                )
                gate.append((jnp.tanh(scores) * weight + weight).astype(BF16))
            gates.append(gate)
        sums = [
            [jnp.dot(gate[pair], value_ref[source, pair], preferred_element_type=F32) for pair in range(pairs)]
            for (source, _), gate in zip(tiles, gates)
        ]
        for (_, target), total in zip(tiles, sums):
            for pair in range(pairs):
                acc_ref[target, pair * wide : (pair + 1) * wide] += total[pair]

    many = found // (2 * UNROLL)

    @pl.loop(0, many)
    def _(index):
        visit(index * (2 * UNROLL), 2 * UNROLL)

    @pl.loop(2 * many, pl.cdiv(found, UNROLL))
    def _(index):
        visit(index * UNROLL, UNROLL)


def start_copies(pairs, sems):
    copies = [pltpu.make_async_copy(a, b, sems.at[i]) for i, (a, b) in enumerate(pairs)]
    for copy in copies:
        copy.start()
    return copies


def query_kernel(nodes_hbm, gain_hbm, wq_hbm, query_ref, nodes_ref, gain_ref, wq_ref, sems):
    for copy in start_copies([(nodes_hbm, nodes_ref), (gain_hbm, gain_ref), (wq_hbm, wq_ref)], sems):
        copy.wait()
    query_ref[...] = scaled_query(rms_scale(nodes_ref[...], gain_ref[...]).astype(BF16), wq_ref)


def make_lists(blocks, source, target, live, list_ref):
    codes, tiles = list_ref.shape[0] // 2, source.shape[1]
    square = (tiles, tiles)
    down, along = lax.broadcasted_iota(jnp.int32, square, 0), lax.broadcasted_iota(jnp.int32, square, 1)
    one = lambda mask: mask.astype(jnp.int32)
    column = lambda row: jnp.sum(jnp.where(down == along, row, 0), axis=1, keepdims=True)
    source_c, target_c = column(source), column(target)
    code, code_c = target // blocks, target_c // blocks
    number, number_c = along[:1], down[:, :1]
    alike = (source == source_c) & (target == target_c)
    rank = jnp.sum(one(alike & (down < along)), axis=0, keepdims=True)
    rank_c = jnp.sum(one(alike & (along < down)), axis=1, keepdims=True)
    first, first_c = (rank % 2 == 0) & (number < live), (rank_c % 2 == 0) & (number_c < live)
    place_c = jnp.sum(one(first & (code == code_c) & (along < down)), axis=1, keepdims=True)
    twin_c = jnp.sum(
        jnp.where(alike & (rank == rank_c + 1) & (number < live), number + 1, 0), axis=1, keepdims=True
    )
    entry_c = number_c + source_c * 1024 + (target_c - code_c * blocks) * (1024 * 1024)
    lane = lax.broadcasted_iota(jnp.int32, (tiles, list_ref.shape[1]), 1)
    here = first_c & (place_c == lane)
    lengths = jnp.zeros((1, list_ref.shape[1]), jnp.int32)
    for each in range(codes):
        mine = here & (code_c == each)
        list_ref[each : each + 1] = jnp.sum(jnp.where(mine, entry_c, 0), axis=0, keepdims=True)
        list_ref[codes + each : codes + each + 1] = jnp.sum(jnp.where(mine, twin_c, 0), axis=0, keepdims=True)
        length = jnp.sum(one(first_c & (code_c == each)), axis=0, keepdims=True)
        lengths += jnp.where(lane[:1] == each, length, 0)
    list_ref[2 * codes :] = lengths


def prepare_kernel(
    blocks, src_hbm, dst_hbm, nodes_hbm, gain_hbm, wk_hbm, wv_hbm, wq_hbm, weight_hbm, live_ref, other_ref,
    key_ref, value_ref, weight_ref, query_ref, gain_ref, wq_ref, list_out,
    nodes_ref, wk_ref, wv_ref, src_ref, dst_ref, sems,
):
    copies = start_copies(
        [
            (src_hbm, src_ref), (dst_hbm, dst_ref), (nodes_hbm, nodes_ref), (gain_hbm, gain_ref), (wk_hbm, wk_ref),
            (wv_hbm, wv_ref), (wq_hbm, wq_ref), (weight_hbm, weight_ref),
        ],
        sems,
    )
    for copy in copies[:2]:
        copy.wait()
    make_lists(blocks, src_ref[...], dst_ref[...], live_ref[0, 0], list_out)
    me = lax.axis_index("col")
    copies[3].wait()
    other = rms_scale(other_ref[...], gain_ref[...]).astype(BF16)
    copies[2].wait()
    normed = rms_scale(nodes_ref[...], gain_ref[...]).astype(BF16)
    copies[4].wait()
    pack_heads(project(normed, wk_ref), key_ref, me * blocks)
    pack_heads(project(other, wk_ref), key_ref, (1 - me) * blocks)
    copies[5].wait()
    pack_heads(project(normed, wv_ref), value_ref, me * blocks)
    pack_heads(project(other, wv_ref), value_ref, (1 - me) * blocks)
    copies[6].wait()
    query_ref[...] = scaled_query(normed, wq_ref)
    copies[7].wait()


def tiles_kernel(
    place, projected, lists_vmem, gain_ref, wq_ref, weight_ref, key_ref, value_ref, block_ref, _, out_ref,
    query_ref, acc_ref, list_ref, sem,
):
    copy = pltpu.make_async_copy(lists_vmem, list_ref, sem)
    copy.start()
    queries = block_ref
    if not projected:
        queries = query_ref
        query_ref[...] = scaled_query(rms_scale(block_ref[...], gain_ref[...]).astype(BF16), wq_ref)
    copy.wait()
    code = HALO + (partner_offset("row", *place) if place else 0)
    sums = out_ref if out_ref.dtype == F32 else acc_ref
    visit_tiles(code, list_ref, weight_ref, queries, key_ref, value_ref, sums)
    if out_ref.dtype != F32:
        out_ref[...] = sums[...].astype(BF16)


def add_kernel(sum_ref, part_ref, out_ref):
    out_ref[...] = sum_ref[...] + part_ref[...].astype(F32)


def last_kernel(nodes_ref, gain_ref, w_out_ref, sum_ref, part_ref, out_ref):
    aggregate = sum_ref[...] + part_ref[...].astype(F32)
    mixed = rms_scale(aggregate, gain_ref[...]).astype(BF16)
    update = jnp.dot(mixed, w_out_ref[...], preferred_element_type=F32)
    out_ref[...] = (nodes_ref[...].astype(F32) + update).astype(BF16)


def local(nodes, ln_gain, w_query, w_key, w_value, w_out, agg_gain, tile_weight, tile_src, tile_dst, tile_live):
    rows_dev, features = nodes.shape
    tile_count, tile_rows = tile_weight.shape[1], tile_weight.shape[-1]
    blocks = rows_dev // tile_rows
    pairs = HEADS // 2
    wide = features // pairs
    sources = lax.axis_size("col") * blocks
    weight = tile_weight[0]
    codes = 2 * HALO + 1
    params = pltpu.CompilerParams(vmem_limit_bytes=32 << 20)

    cost = pl.CostEstimate(flops=1 << 20, bytes_accessed=1 << 16, transcendentals=0)
    shape = jax.ShapeDtypeStruct
    block_bf16 = shape((rows_dev, features), BF16)
    block_f32 = shape((rows_dev, features), F32)
    packed = shape((sources, pairs, 2 * tile_rows, wide), BF16)
    lists = (2 * codes + 1, 128)
    assert tile_count + UNROLL <= 128 and sources <= 1024
    square = pltpu.VMEM((features, features), BF16)

    def in_hbm(*arrays):
        return [pltpu.with_memory_space_constraint(array, pltpu.HBM) for array in arrays]

    near, diagonal = (1, 0), (1, 1)
    places = (near, (HALO, 1), (HALO, 0), diagonal)
    other = lax.ppermute(nodes, "col", [(0, 1), (1, 0)])
    arrived = {near: swap(nodes, "row", *near)}
    early = pl.pallas_call(
        query_kernel,
        out_shape=block_bf16,
        in_specs=[HBM] * 3,
        out_specs=VMEM,
        scratch_shapes=[
            pltpu.VMEM((rows_dev, features), BF16), pltpu.VMEM((1, features), F32), square,
            pltpu.SemaphoreType.DMA((3,)),
        ],
        compiler_params=params,
        cost_estimate=cost,
        name="query",
    )(*in_hbm(nodes, ln_gain.reshape(1, features), w_query))
    for place in places[1:3]:
        arrived[place] = swap(early, "row", *place)

    keys, values, weight_held, query, gain, wq, lists_out = pl.pallas_call(
        functools.partial(prepare_kernel, blocks),
        out_shape=(
            packed, packed, shape(weight.shape, BF16), block_bf16, shape((1, features), F32),
            shape(w_query.shape, BF16), shape(lists, jnp.int32),
        ),
        in_specs=[HBM] * 8 + [SMEM, VMEM],
        out_specs=(VMEM,) * 7,
        scratch_shapes=[
            pltpu.VMEM((rows_dev, features), BF16), square, square, pltpu.VMEM(tile_src.shape, jnp.int32),
            pltpu.VMEM(tile_dst.shape, jnp.int32), pltpu.SemaphoreType.DMA((9,)),
        ],
        compiler_params=params,
        cost_estimate=cost,
        name="prepare",
    )(
        *in_hbm(tile_src, tile_dst, nodes, ln_gain.reshape(1, features), w_key, w_value, w_query, weight),
        tile_live,
        other,
    )

    arrived[diagonal] = swap(query, "row", *diagonal)

    def tiles(name, place, projected, block, after, out):
        return pl.pallas_call(
            functools.partial(tiles_kernel, place, projected),
            out_shape=out,
            in_specs=[VMEM] * 7 + [ANY],
            out_specs=VMEM,
            scratch_shapes=[
                pltpu.VMEM((rows_dev, features), BF16), pltpu.VMEM((rows_dev, features), F32),
                pltpu.SMEM(lists, jnp.int32), pltpu.SemaphoreType.DMA,
            ],
            compiler_params=params,
            cost_estimate=cost,
            name=name,
        )(lists_out, gain, wq, weight_held, keys, values, block, after)

    last, returned = gain, []
    for place in places:
        last = tiles("tiles_%d_%d" % place, place, place != near, arrived[place], last, block_bf16)
        returned.append(swap(last, "row", *place))
    total = tiles("own_tiles", None, True, query, last, block_f32)
    for part in returned[:-1]:
        total = pl.pallas_call(
            add_kernel,
            out_shape=block_f32,
            in_specs=[VMEM] * 2,
            out_specs=VMEM,
            input_output_aliases={0: 0},
            compiler_params=params,
            cost_estimate=pl.CostEstimate(flops=1 << 18, bytes_accessed=2 << 20, transcendentals=0),
            name="add",
        )(total, part)

    return pl.pallas_call(
        last_kernel,
        out_shape=block_bf16,
        in_specs=[VMEM] * 5,
        out_specs=VMEM,
        compiler_params=params,
        cost_estimate=cost,
        name="mix",
    )(nodes, agg_gain.reshape(1, features), w_out, total, returned[-1])


def solution(mesh):
    return jax.shard_map(
        local,
        mesh=mesh,
        in_specs=(
            P(("slide", "row", "col"), None),
            P(),
            P(),
            P(),
            P(),
            P(),
            P(),
            P(("slide", "row"), "col", None, None),
            P(("slide", "row"), "col"),
            P(("slide", "row"), "col"),
            P(("slide", "row"), "col"),
        ),
        out_specs=P(("slide", "row", "col"), None),
        check_vma=False,
    )
```
